32 devices in a mesh: tm: 8 (over z, core), neuron: 4 (over y, x).
Axes of the slice: x: 2, y: 2, z: 4, core: 2. Of those that a mesh axis runs over, the one named last changes fastest.
Arguments:
- observations: bfloat16 [1024, 12800], P('tm', 'neuron'), may hold values from -6 to 6
- loadings: bfloat16 [512, 12800], P(None, 'neuron'), may hold values from -0.01953125 to 0.01953125
- region_mask: int32 [4, 100], P(None, 'neuron'), may hold values 0 or 1
- precision: float32 [12800], P('neuron'), may hold values from 0.5 to 8
- decay_rate: bfloat16 [1024, 512], P('tm'), may hold values from 9.667969e-05 to 0.42
- smoothing_lag: float32 [512], replicated, may hold values from 0.5 to 1.25
Outputs:
- loading_grad: bfloat16 [512, 12800], P('tm', 'neuron')
The draws below stay inside these ranges and needn't reach their ends.
All inputs are finite; a program needn't handle non-finite values. No bound on the sum of `region_mask` on one device may be relied on, other than what follows from the above.
Results may differ from the reference program's by a relative error of at most 0.0064.
Values may be sent and summed in bfloat16 or wider, within the bound.
A program may use at most 128 MiB of HBM per device.

```python
import math
import jax
import jax.numpy as jnp
from jax import lax

S = 512
LATENT_GROUP = 128
REGION = 128
FR = 128
TIME = 1024
NEUR = 12800
GROUPS = 4
REGIONS = 100
N_TM = 8


def draw_decay_rate(key, part):
    divided_seed_tokens = jax.random.split(key, 6)
    slow_share = 5
    slow_mask = jax.random.randint(divided_seed_tokens[0], (S,), 0, 10) < slow_share
    fast_rate = jnp.exp(jax.random.uniform(divided_seed_tokens[1], (S,), jnp.float32, math.log(1.0 / 25.0), math.log(1.0 / 15.0)))
    slow_rate = jax.random.uniform(divided_seed_tokens[2], (S,), jnp.float32, 0.2, 0.6) / TIME
    resting_spike_level = jnp.where(slow_mask, slow_rate, fast_rate)
    scaling_factor = jax.random.uniform(divided_seed_tokens[3], (TIME // FR, S), jnp.float32, 0.5, 1.0)
    scaling_factor = jnp.repeat(scaling_factor, FR, axis=0)
    tertile_span = TIME // 3
    surge_step_total = jnp.arange(3) * tertile_span + jax.random.randint(divided_seed_tokens[4], (3,), 0, tertile_span)
    surge_magnitude = jax.random.uniform(divided_seed_tokens[5], (3,), jnp.float32, 0.22, 0.35)
    step_ordinal = jnp.arange(TIME)
    surge_spike_level = jnp.sum(jnp.where(step_ordinal[:, None] == surge_step_total[None, :], surge_magnitude[None, :], 0.0), axis=1)
    return (resting_spike_level[None, :] * scaling_factor + surge_spike_level[:, None]).astype(jnp.float32).astype(jnp.bfloat16)


def touch_ends(result, own_key, smallest, high):
    index_at = [jax.random.randint(jax.random.fold_in(own_key, axis), (), 0, length) for axis, length in enumerate(result.shape)]
    main_axis = result.shape.index(max(result.shape))
    beside = index_at[:main_axis] + [(index_at[main_axis] + 1) % result.shape[main_axis]] + index_at[main_axis + 1:]
    return result.at[tuple(index_at)].set(smallest).at[tuple(beside)].set(high)


def levels(key, shape, shards, low, largest):
    factor_of = 1.0
    for axis_at, blocks in shards:
        steps = jax.random.uniform(jax.random.fold_in(jax.random.fold_in(key, 6), axis_at), (blocks,), jnp.float32, low / len(shards), largest / len(shards))
        factor_of = factor_of * jnp.repeat(jnp.exp(steps), shape[axis_at] // blocks).reshape((-1,) + (1,) * (len(shape) - 1 - axis_at))
    return factor_of


def centred(stream_key, shape, scale, limit, shards=(), kind=jnp.bfloat16):
    array = jax.random.normal(stream_key, shape, jnp.float32) * scale
    if len(shards) > 0:
        array = levels(stream_key, shape, shards, -0.22, 0.18) * array
    return jnp.clip(array, min=-limit, max=limit).astype(kind)


def setup_inputs(seed: int = 0) -> dict:
    streams_of = jax.random.split(jax.random.key(seed), 7)
    observations = centred(streams_of[0], (TIME, NEUR), 1.0, 6.0, ((0, 8), (1, 4)))
    loadings = centred(streams_of[1], (S, NEUR), (NEUR * 8) ** -0.5, 0.01953125, ((1, 4),))
    region_mask = touch_ends((jax.random.randint(streams_of[2], (GROUPS, REGIONS), 0, 4) < 3).astype(jnp.int32), jax.random.fold_in(streams_of[2], 1), 0, 1)
    precision = jnp.clip(jnp.exp(math.log(8.0) - 2.7725887 * jax.random.uniform(streams_of[3], (NEUR,), jnp.float32) ** levels(streams_of[3], (NEUR,), ((0, 4),), -0.2, 0.2)), 0.5, 8.0)
    decay_rate = draw_decay_rate(jax.random.fold_in(streams_of[6], 71), 0)
    smoothing_lag = jnp.clip(jax.random.uniform(streams_of[5], (S,), jnp.float32, 0.5, 1.25), 0.5, 1.25)
    return {"observations": observations, "loadings": loadings, "region_mask": region_mask, "precision": precision, "decay_rate": decay_rate, "smoothing_lag": smoothing_lag}


def combine(earlier, latter):
    return (earlier[0] * latter[0], latter[0] * earlier[1] + latter[1])

def reference(observations, loadings, region_mask, precision, decay_rate, smoothing_lag):
    mask_full = jnp.broadcast_to(region_mask[:, None, :, None], (GROUPS, LATENT_GROUP, REGIONS, REGION)).reshape(S, NEUR).astype(jnp.bfloat16)
    effective = loadings * mask_full
    weighted = (effective.astype(jnp.float32) * precision[None, :]).astype(jnp.bfloat16)
    driving = jnp.dot(observations, weighted.T, preferred_element_type=jnp.float32)
    rate_field = decay_rate.astype(jnp.float32)
    decays = jnp.exp(-rate_field)
    innovation = jnp.sqrt(-jnp.expm1(-2.0 * rate_field))
    unused_mult, filtered = lax.associative_scan(combine, (decays, innovation * driving), axis=0)
    retained = jnp.exp(-rate_field * smoothing_lag[None, :])
    back_mult, back_add = lax.associative_scan(combine, (retained[::-1], ((1.0 - retained) * filtered)[::-1]), axis=0)
    smoothed = back_add[::-1].astype(jnp.bfloat16)
    blocks_obs = observations.reshape(N_TM, FR, NEUR)
    blocks_smooth = smoothed.reshape(N_TM, FR, S)

    def advance(running, pieces):
        frames_obs, frames_smooth = pieces
        rebuilt = jnp.dot(frames_smooth, effective, preferred_element_type=jnp.float32)
        residual = ((frames_obs.astype(jnp.float32) - rebuilt) * precision[None, :]).astype(jnp.bfloat16)
        product = lax.dot_general(frames_smooth, residual, (((0,), (0,)), ((), ())), preferred_element_type=jnp.float32)
        return (running + product, None)
    summed, unused_out = lax.scan(advance, jnp.zeros((S, NEUR), jnp.float32), (blocks_obs, blocks_smooth))
    return (summed * (1.0 / math.sqrt(TIME)) * mask_full.astype(jnp.float32)).astype(jnp.bfloat16)
```

```python
import functools
import math

import jax
import jax.numpy as jnp
from jax import lax
from jax.experimental import pallas as pl
from jax.experimental.pallas import tpu as pltpu
from jax.sharding import PartitionSpec as P

LATENT_GROUP = 128
REGION = 128
CORES = 2
SUB = 8
F32 = jnp.float32
BF16 = jnp.bfloat16


def one_minus_exp_neg(x):
    series = jnp.full_like(x, 1.0 / 10.0)
    for n in range(9, 0, -1):
        series = (1.0 - x * series) * (1.0 / n)
    return jnp.where(x < 0.5, x * series, 1.0 - jnp.exp(-x))


def kernel(
    NT,
    NN,
    obs_ref,
    load_ref,
    mask_ref,
    prec_ref,
    rate_ref,
    lag_ref,
    out_ref,
    obs_all,
    weight,
    acc,
    drv_out,
    drv_in,
    dec_s,
    ret_s,
    x_s,
    parts,
    summ,
    enter_s,
    follow_s,
    sm_all,
    sm_t,
    out_s,
    obs_ss,
    obs_rs,
    drv_ss,
    drv_rs,
    summ_ss,
    summ_rs,
    sa_ss,
    sb_ss,
    sc_ss,
    sm_rs,
    out_ss,
    out_rs,
):
    frames, neurons = obs_ref.shape
    latents = load_ref.shape[0]
    groups, regions = mask_ref.shape
    LN = latents // NN
    LO = latents // NT
    NZ = NT // CORES
    steps = frames // SUB
    smin, smax = regions // NT, -(-regions // NT)
    me = lax.axis_index("tm")
    j = lax.axis_index("neuron")
    z, core = me // CORES, lax.rem(me, CORES)
    partner = z * CORES + 1 - core

    def first(o):
        return (o * regions + NT - 1) // NT

    def count(o):
        return first(o + 1) - first(o)

    def tm_at(d):
        return lax.rem(me + d, NT)

    def nn_at(d):
        return lax.rem(j + d, NN)

    def cols(r):
        return pl.ds(pl.multiple_of(r * REGION, REGION), REGION)

    def rows(b, n):
        return pl.ds(pl.multiple_of(b * n, n), n)

    def remote(src, dst, ss, rs, tm=None, nn=None):
        return pltpu.make_async_remote_copy(
            src_ref=src,
            dst_ref=dst,
            send_sem=ss,
            recv_sem=rs,
            device_id={"tm": me if tm is None else tm, "neuron": j if nn is None else nn},
            device_id_type=pl.DeviceIdType.MESH,
        )

    def guarded(s, owner, body):
        if s < smin:
            body()
        else:
            pl.when(s < count(owner))(body)

    barrier = pltpu.get_barrier_semaphore()
    for d in range(1, NT):
        pl.semaphore_signal(
            barrier, inc=1, device_id={"tm": tm_at(d), "neuron": j},
            device_id_type=pl.DeviceIdType.MESH,
        )
    for d in range(1, NN):
        pl.semaphore_signal(
            barrier, inc=1, device_id={"tm": me, "neuron": nn_at(d)},
            device_id_type=pl.DeviceIdType.MESH,
        )
    pl.semaphore_wait(barrier, NT + NN - 2)

    def obs_copy(s, d):
        o = tm_at(d)
        return remote(
            obs_ref.at[:, cols(first(o) + s)],
            obs_all.at[s, rows(me, frames), :],
            obs_ss.at[d, s],
            obs_rs.at[me, s],
            tm=o,
        )

    for s in range(smax):
        for d in range(1, NT):
            guarded(s, tm_at(d), lambda: obs_copy(s, d).start())

    per = 5 if regions % 5 == 0 else 1
    acc[...] = jnp.zeros_like(acc)

    def mask_value(g, r):
        return mask_ref[g, r].astype(F32)

    def effective(g, r):
        block = load_ref[pl.ds(g * LATENT_GROUP, LATENT_GROUP), cols(r)].astype(F32)
        return block * mask_value(g, r)

    @pl.loop(0, regions // per)
    def _(c):
        for q in range(per):
            r = c * per + q
            p_row = prec_ref[:, cols(r)]
            for g in range(groups):
                weight[pl.ds(g * LATENT_GROUP, LATENT_GROUP), pl.ds(q * REGION, REGION)] = (
                    effective(g, r) * p_row
                ).astype(BF16)
        width = per * REGION
        acc[...] += lax.dot_general(
            obs_ref[:, pl.ds(pl.multiple_of(c * width, width), width)],
            weight[...],
            (((1,), (1,)), ((), ())),
            preferred_element_type=F32,
        )

    def drv_copy(d):
        g = nn_at(d)
        return remote(
            drv_out.at[g], drv_in.at[j], drv_ss.at[d], drv_rs.at[j], nn=g
        )

    for g in range(NN):
        drv_out[g] = acc[:, g * LN : (g + 1) * LN]
    for d in range(1, NN):
        drv_copy(d).start()
    drv_in[j] = drv_out[j]

    rate = jnp.zeros((frames, LN), F32)
    lag = jnp.zeros((1, LN), F32)
    for g in range(NN):
        mine = j == g
        rate = jnp.where(mine, rate_ref[:, g * LN : (g + 1) * LN].astype(F32), rate)
        lag = jnp.where(mine, lag_ref[:, g * LN : (g + 1) * LN], lag)
    dec_s[...] = jnp.exp(-rate)
    ret_s[...] = jnp.exp(-(rate * lag))
    innovation = jnp.sqrt(one_minus_exp_neg(2.0 * rate))

    for d in range(1, NN):
        g = nn_at(d)
        remote(drv_out.at[g], drv_in.at[g], drv_ss.at[d], drv_rs.at[g], nn=g).wait_recv()
    total = drv_in[0]
    for g in range(1, NN):
        total = total + drv_in[g]
    x_s[...] = innovation * total

    def at(ref, i):
        return ref[pl.ds(i, SUB, stride=steps), :]

    mult = jnp.ones((SUB, LN), F32)
    add = jnp.zeros((SUB, LN), F32)
    fwd = []
    for i in range(steps):
        dec = at(dec_s, i)
        mult = dec * mult
        add = dec * add + at(x_s, i)
        fwd.append((mult, add))
    pm, pa = [jnp.ones((1, LN), F32)], [jnp.zeros((1, LN), F32)]
    for s in range(SUB):
        pm.append(mult[s : s + 1] * pm[-1])
        pa.append(mult[s : s + 1] * pa[-1] + add[s : s + 1])
    pm_all = jnp.concatenate(pm[:SUB], axis=0)
    pa_all = jnp.concatenate(pa[:SUB], axis=0)
    rm = jnp.ones((SUB, LN), F32)
    sv = jnp.zeros((SUB, LN), F32)
    uv = jnp.zeros((SUB, LN), F32)
    bwd = [None] * steps
    for i in reversed(range(steps)):
        ret = at(ret_s, i)
        m_i, a_i = fwd[i]
        keep = 1.0 - ret
        rm = ret * rm
        sv = ret * sv + keep * (a_i + m_i * pa_all)
        uv = ret * uv + keep * (m_i * pm_all)
        bwd[i] = (rm, sv, uv)
    rr, ss, uu = (
        [jnp.ones((1, LN), F32)],
        [jnp.zeros((1, LN), F32)],
        [jnp.zeros((1, LN), F32)],
    )
    for s in reversed(range(SUB)):
        r_s = rm[s : s + 1]
        rr.append(r_s * rr[-1])
        ss.append(r_s * ss[-1] + sv[s : s + 1])
        uu.append(r_s * uu[-1] + uv[s : s + 1])
    rr_all = jnp.concatenate(rr[:SUB][::-1], axis=0)
    ss_all = jnp.concatenate(ss[:SUB][::-1], axis=0)
    uu_all = jnp.concatenate(uu[:SUB][::-1], axis=0)
    zero = jnp.zeros((1, LN), F32)
    summ[me] = jnp.concatenate(
        [pm[SUB], pa[SUB], rr[SUB], ss[SUB], uu[SUB], zero, zero, zero], axis=0
    )

    def summ_copy(d):
        o = tm_at(d)
        return remote(summ.at[me], summ.at[me], summ_ss.at[d], summ_rs.at[me], tm=o)

    for d in range(1, NT):
        summ_copy(d).start()
    for i in range(steps):
        rm_i, s_i, u_i = bwd[i]
        parts[0, i] = s_i + rm_i * ss_all
        parts[1, i] = u_i + rm_i * uu_all
        parts[2, i] = rm_i * rr_all
    for d in range(1, NT):
        o = tm_at(d)
        remote(summ.at[o], summ.at[o], summ_ss.at[d], summ_rs.at[o], tm=o).wait_recv()

    entering = [zero]
    for b in range(NT):
        enter_s[b] = jnp.broadcast_to(entering[b], (SUB, LN))
        entering.append(summ[b, 0:1] * entering[b] + summ[b, 1:2])
    following = zero
    for b in reversed(range(NT)):
        follow_s[b] = jnp.broadcast_to(following, (SUB, LN))
        following = summ[b, 2:3] * following + summ[b, 3:4] + summ[b, 4:5] * entering[b]
    e_me, f_me = enter_s[me], follow_s[me]
    for i in range(steps):
        x_s[pl.ds(i, SUB, stride=steps), :] = parts[0, i] + parts[1, i] * e_me + parts[2, i] * f_me
    sm_all[j, rows(me, frames), :] = x_s[...].astype(BF16)

    def block(g, b):
        return sm_all.at[g, rows(b, frames), :]

    def z_at(d):
        return lax.rem(z + d, NZ) * CORES + core

    def send_z(d):
        return remote(block(j, me), block(j, me), sa_ss.at[d], sm_rs.at[me, j], tm=z_at(d))

    def send_n(dz, d):
        b = z_at(dz)
        return remote(block(j, b), block(j, b), sb_ss.at[dz, d], sm_rs.at[b, j], nn=nn_at(d))

    def send_c(dz, d):
        b, g = z_at(dz), nn_at(d)
        return remote(block(g, b), block(g, b), sc_ss.at[dz, d], sm_rs.at[b, g], tm=partner)

    def arrive(b, g):
        remote(block(g, b), block(g, b), sa_ss.at[0], sm_rs.at[b, g], tm=partner).wait_recv()

    def turn(b, g):
        sm_t[g, :, rows(b, frames)] = sm_all[g, rows(b, frames), :].T

    for d in range(1, NZ):
        send_z(d).start()
    for dz in range(NZ):
        if dz > 0:
            arrive(z_at(dz), j)
        for d in range(1, NN):
            send_n(dz, d).start()
        send_c(dz, 0).start()
    for dz in range(NZ):
        turn(z_at(dz), j)
    for dz in range(NZ):
        for d in range(1, NN):
            g = nn_at(d)
            arrive(z_at(dz), g)
            send_c(dz, d).start()
            turn(z_at(dz), g)
    for dz in range(NZ):
        for d in range(NN):
            b = lax.rem(z + dz, NZ) * CORES + 1 - core
            arrive(b, nn_at(d))
            turn(b, nn_at(d))

    scale = 1.0 / math.sqrt(frames * NT)
    obs_all_own = []
    for s in range(smax):
        guarded(
            s,
            me,
            lambda: obs_all.__setitem__(
                (s, rows(me, frames), slice(None)), obs_ref[:, cols(first(me) + s)]
            ),
        )

    def out_copy(s, d):
        o = tm_at(d)
        return remote(
            out_s.at[s, rows(o, LO), :],
            out_ref.at[:, cols(first(me) + s)],
            out_ss.at[d, s],
            out_rs.at[me, s],
            tm=o,
        )

    def slot(s):
        r = first(me) + s
        for d in range(1, NT):
            o = tm_at(d)
            there = obs_all.at[s, rows(o, frames), :]
            remote(there, there, obs_ss.at[d, s], obs_rs.at[o, s], tm=o).wait_recv()
        eff = jnp.concatenate([effective(g, r) for g in range(groups)], axis=0).astype(BF16)
        smooth = jnp.concatenate([sm_all[g] for g in range(NN)], axis=1)
        rebuilt = jnp.dot(smooth, eff, preferred_element_type=F32)
        residual = ((obs_all[s].astype(F32) - rebuilt) * prec_ref[:, cols(r)]).astype(BF16)
        smooth_t = sm_t[...].reshape(latents, NT * frames)
        summed = jnp.dot(smooth_t, residual, preferred_element_type=F32) * scale
        for g in range(groups):
            out_s[s, pl.ds(g * LATENT_GROUP, LATENT_GROUP), :] = (
                summed[g * LATENT_GROUP : (g + 1) * LATENT_GROUP] * mask_value(g, r)
            ).astype(BF16)
        for d in range(1, NT):
            out_copy(s, d).start()
        out_ref[:, cols(r)] = out_s[s, rows(me, LO), :]

    for s in range(smax):
        guarded(s, me, lambda: slot(s))

    for s in range(smax):
        for d in range(1, NT):
            o = tm_at(d)

            def landed():
                there = out_ref.at[:, cols(first(o) + s)]
                remote(there, there, out_ss.at[d, s], out_rs.at[o, s], tm=o).wait_recv()

            guarded(s, o, landed)

    for d in range(1, NT):
        summ_copy(d).wait_send()
        for s in range(smax):
            guarded(s, tm_at(d), lambda: obs_copy(s, d).wait_send())
            guarded(s, me, lambda: out_copy(s, d).wait_send())
    for d in range(1, NN):
        drv_copy(d).wait_send()
    for d in range(1, NZ):
        send_z(d).wait_send()
    for dz in range(NZ):
        for d in range(1, NN):
            send_n(dz, d).wait_send()
        for d in range(NN):
            send_c(dz, d).wait_send()


def per_device(NT, NN, observations, loadings, region_mask, precision, decay_rate, smoothing_lag):
    frames, neurons = observations.shape
    latents = loadings.shape[0]
    regions = region_mask.shape[1]
    LN, LO, NZ = latents // NN, latents // NT, NT // CORES
    smax = -(-regions // NT)
    steps = frames // SUB
    per = 5 if regions % 5 == 0 else 1
    dma = pltpu.SemaphoreType.DMA
    vm = pl.BlockSpec(memory_space=pltpu.VMEM)
    return pl.pallas_call(
        functools.partial(kernel, NT, NN),
        out_shape=jax.ShapeDtypeStruct((LO, neurons), BF16),
        in_specs=[vm, vm, pl.BlockSpec(memory_space=pltpu.SMEM), vm, vm, vm],
        out_specs=vm,
        scratch_shapes=[
            pltpu.VMEM((smax, NT * frames, REGION), BF16),
            pltpu.VMEM((latents, per * REGION), BF16),
            pltpu.VMEM((frames, latents), F32),
            pltpu.VMEM((NN, frames, LN), F32),
            pltpu.VMEM((NN, frames, LN), F32),
            pltpu.VMEM((frames, LN), F32),
            pltpu.VMEM((frames, LN), F32),
            pltpu.VMEM((frames, LN), F32),
            pltpu.VMEM((3, steps, SUB, LN), F32),
            pltpu.VMEM((NT, SUB, LN), F32),
            pltpu.VMEM((NT, SUB, LN), F32),
            pltpu.VMEM((NT, SUB, LN), F32),
            pltpu.VMEM((NN, NT * frames, LN), BF16),
            pltpu.VMEM((NN, LN, NT * frames), BF16),
            pltpu.VMEM((smax, latents, REGION), BF16),
            dma((NT, smax)),
            dma((NT, smax)),
            dma((NN,)),
            dma((NN,)),
            dma((NT,)),
            dma((NT,)),
            dma((NZ,)),
            dma((NZ, NN)),
            dma((NZ, NN)),
            dma((NT, NN)),
            dma((NT, smax)),
            dma((NT, smax)),
        ],
        compiler_params=pltpu.CompilerParams(
            collective_id=0, has_side_effects=True, vmem_limit_bytes=48 * 1024 * 1024
        ),
    )(
        observations,
        loadings,
        region_mask,
        precision.reshape(1, neurons),
        decay_rate,
        smoothing_lag.reshape(1, latents),
    )


def solution(mesh):
    return jax.shard_map(
        functools.partial(per_device, mesh.shape["tm"], mesh.shape["neuron"]),
        mesh=mesh,
        in_specs=(
            P("tm", "neuron"),
            P(None, "neuron"),
            P(None, "neuron"),
            P("neuron"),
            P("tm", None),
            P(),
        ),
        out_specs=P("tm", "neuron"),
        check_vma=False,
    )
```

```python
import functools
import math

import jax
import jax.numpy as jnp
from jax import lax
from jax.experimental import pallas as pl
from jax.experimental.pallas import tpu as pltpu
from jax.sharding import PartitionSpec as P

LATENT_GROUP = 128
REGION = 128
CORES = 2
EARLY = 2
SUB = 8
F32 = jnp.float32
BF16 = jnp.bfloat16


def one_minus_exp_neg(x):
    series = jnp.full_like(x, 1.0 / 10.0)
    for n in range(9, 0, -1):
        series = (1.0 - x * series) * (1.0 / n)
    return jnp.where(x < 0.5, x * series, 1.0 - jnp.exp(-x))


def kernel(
    NT,
    NN,
    obs_hbm,
    load_hbm,
    mask_hbm,
    prec_hbm,
    rate_hbm,
    lag_hbm,
    out_ref,
    obs_ref,
    load_ref,
    mask_ref,
    prec_ref,
    rate_ref,
    lag_ref,
    in_sem,
    load_sem,
    obs_all,
    weight,
    acc,
    drv_out,
    drv_in,
    dec_s,
    ret_s,
    x_s,
    parts,
    summ,
    enter_s,
    follow_s,
    sm_all,
    sm_t,
    out_s,
    obs_ss,
    obs_rs,
    drv_ss,
    drv_rs,
    summ_ss,
    summ_rs,
    sa_ss,
    sb_ss,
    sc_ss,
    sm_rs,
    out_ss,
    out_rs,
):
    frames, neurons = obs_ref.shape
    latents = load_ref.shape[0]
    groups, regions = mask_ref.shape
    LN = latents // NN
    LO = latents // NT
    NZ = NT // CORES
    steps = frames // SUB
    smin, smax = regions // NT, -(-regions // NT)
    me = lax.axis_index("tm")
    j = lax.axis_index("neuron")
    z, core = me // CORES, lax.rem(me, CORES)
    partner = z * CORES + 1 - core

    def first(o):
        return (o * regions + NT - 1) // NT

    def count(o):
        return first(o + 1) - first(o)

    def peer(i, d, n):
        if n & (n - 1):
            return lax.rem(i + d, n)
        bit = 1
        while bit < n:
            if d & bit:
                i = i + bit - 2 * bit * lax.rem(i // bit, 2)
            bit *= 2
        return i

    def tm_at(d):
        return peer(me, d, NT)

    def nn_at(d):
        return peer(j, d, NN)

    def cols(r):
        return pl.ds(pl.multiple_of(r * REGION, REGION), REGION)

    def rows(b, n):
        return pl.ds(pl.multiple_of(b * n, n), n)

    def remote(src, dst, ss, rs, tm=None, nn=None):
        return pltpu.make_async_remote_copy(
            src_ref=src,
            dst_ref=dst,
            send_sem=ss,
            recv_sem=rs,
            device_id={"tm": me if tm is None else tm, "neuron": j if nn is None else nn},
            device_id_type=pl.DeviceIdType.MESH,
        )

    def guarded(s, owner, body):
        if s < smin:
            body()
        else:
            pl.when(s < count(owner))(body)

    per = 5 if regions % 5 == 0 else 1
    width = per * REGION

    def load_copy(c):
        where = pl.ds(pl.multiple_of(c * width, width), width)
        return pltpu.make_async_copy(load_hbm.at[:, where], load_ref.at[:, where], load_sem.at[c])

    inputs = [
        pltpu.make_async_copy(a, b, in_sem.at[i])
        for i, (a, b) in enumerate(
            [
                (mask_hbm, mask_ref),
                (prec_hbm, prec_ref),
                (obs_hbm, obs_ref),
                (rate_hbm, rate_ref),
                (lag_hbm, lag_ref),
            ]
        )
    ]
    for copy in inputs[:3]:
        copy.start()
    for c in range(regions // per):
        load_copy(c).start()
    for copy in inputs[3:]:
        copy.start()

    barrier = pltpu.get_barrier_semaphore()
    for d in range(1, NT):
        pl.semaphore_signal(
            barrier, inc=1, device_id={"tm": tm_at(d), "neuron": j},
            device_id_type=pl.DeviceIdType.MESH,
        )
    for d in range(1, NN):
        pl.semaphore_signal(
            barrier, inc=1, device_id={"tm": me, "neuron": nn_at(d)},
            device_id_type=pl.DeviceIdType.MESH,
        )
    pl.semaphore_wait(barrier, NT + NN - 2)

    def obs_copy(s, d):
        o = tm_at(d)
        return remote(
            obs_hbm.at[:, cols(first(o) + s)],
            obs_all.at[s, rows(me, frames), :],
            obs_ss.at[d, s],
            obs_rs.at[me, s],
            tm=o,
        )

    def send_obs(slots):
        for s in slots:
            for d in range(1, NT):
                guarded(s, tm_at(d), lambda: obs_copy(s, d).start())

    early = min(EARLY, smax)
    send_obs(range(early))

    for copy in inputs[:3]:
        copy.wait()
    acc[...] = jnp.zeros_like(acc)

    def mask_value(g, r):
        return mask_ref[g, r].astype(F32)

    def effective(g, r):
        block = load_ref[pl.ds(g * LATENT_GROUP, LATENT_GROUP), cols(r)].astype(F32)
        return block * mask_value(g, r)

    @pl.loop(0, regions // per)
    def _(c):
        load_copy(c).wait()
        for q in range(per):
            r = c * per + q
            p_row = prec_ref[pl.ds(r, 1), :]
            for g in range(groups):
                weight[pl.ds(g * LATENT_GROUP, LATENT_GROUP), pl.ds(q * REGION, REGION)] = (
                    effective(g, r) * p_row
                ).astype(BF16)
        acc[...] += lax.dot_general(
            obs_ref[:, pl.ds(pl.multiple_of(c * width, width), width)],
            weight[...],
            (((1,), (1,)), ((), ())),
            preferred_element_type=F32,
        )

    def drv_copy(d):
        g = nn_at(d)
        return remote(
            drv_out.at[g], drv_in.at[j], drv_ss.at[d], drv_rs.at[j], nn=g
        )

    for g in range(NN):
        drv_out[g] = acc[:, g * LN : (g + 1) * LN].astype(BF16)
    for d in range(1, NN):
        drv_copy(d).start()
    for copy in inputs[3:]:
        copy.wait()
    own = jnp.zeros((frames, LN), F32)
    rate = jnp.zeros((frames, LN), F32)
    lag = jnp.zeros((1, LN), F32)
    for g in range(NN):
        mine = j == g
        own = jnp.where(mine, acc[:, g * LN : (g + 1) * LN], own)
        rate = jnp.where(mine, rate_ref[:, g * LN : (g + 1) * LN].astype(F32), rate)
        lag = jnp.where(mine, lag_ref[:, g * LN : (g + 1) * LN], lag)
    dec_s[...] = jnp.exp(-rate)
    ret_s[...] = jnp.exp(-(rate * lag))
    innovation = jnp.sqrt(one_minus_exp_neg(2.0 * rate))

    for d in range(1, NN):
        g = nn_at(d)
        remote(drv_out.at[g], drv_in.at[g], drv_ss.at[d], drv_rs.at[g], nn=g).wait_recv()
    total = own
    for d in range(1, NN):
        total = total + drv_in[nn_at(d)].astype(F32)
    x_s[...] = innovation * total

    def at(ref, i):
        return ref[pl.ds(i, SUB, stride=steps), :]

    mult = jnp.ones((SUB, LN), F32)
    add = jnp.zeros((SUB, LN), F32)
    fwd = []
    for i in range(steps):
        dec = at(dec_s, i)
        mult = dec * mult
        add = dec * add + at(x_s, i)
        fwd.append((mult, add))
    pm, pa = [jnp.ones((1, LN), F32)], [jnp.zeros((1, LN), F32)]
    for s in range(SUB):
        pm.append(mult[s : s + 1] * pm[-1])
        pa.append(mult[s : s + 1] * pa[-1] + add[s : s + 1])
    pm_all = jnp.concatenate(pm[:SUB], axis=0)
    pa_all = jnp.concatenate(pa[:SUB], axis=0)
    rm = jnp.ones((SUB, LN), F32)
    sv = jnp.zeros((SUB, LN), F32)
    uv = jnp.zeros((SUB, LN), F32)
    bwd = [None] * steps
    for i in reversed(range(steps)):
        ret = at(ret_s, i)
        m_i, a_i = fwd[i]
        keep = 1.0 - ret
        rm = ret * rm
        sv = ret * sv + keep * (a_i + m_i * pa_all)
        uv = ret * uv + keep * (m_i * pm_all)
        bwd[i] = (rm, sv, uv)
    rr, ss, uu = (
        [jnp.ones((1, LN), F32)],
        [jnp.zeros((1, LN), F32)],
        [jnp.zeros((1, LN), F32)],
    )
    for s in reversed(range(SUB)):
        r_s = rm[s : s + 1]
        rr.append(r_s * rr[-1])
        ss.append(r_s * ss[-1] + sv[s : s + 1])
        uu.append(r_s * uu[-1] + uv[s : s + 1])
    rr_all = jnp.concatenate(rr[:SUB][::-1], axis=0)
    ss_all = jnp.concatenate(ss[:SUB][::-1], axis=0)
    uu_all = jnp.concatenate(uu[:SUB][::-1], axis=0)
    zero = jnp.zeros((1, LN), F32)
    summ[me] = jnp.concatenate(
        [pm[SUB], pa[SUB], rr[SUB], ss[SUB], uu[SUB], zero, zero, zero], axis=0
    )

    def summ_copy(d):
        o = tm_at(d)
        return remote(summ.at[me], summ.at[me], summ_ss.at[d], summ_rs.at[me], tm=o)

    for d in range(1, NT):
        summ_copy(d).start()
    for i in range(steps):
        rm_i, s_i, u_i = bwd[i]
        parts[0, i] = s_i + rm_i * ss_all
        parts[1, i] = u_i + rm_i * uu_all
        parts[2, i] = rm_i * rr_all
    for d in range(1, NT):
        o = tm_at(d)
        remote(summ.at[o], summ.at[o], summ_ss.at[d], summ_rs.at[o], tm=o).wait_recv()

    entering = [zero]
    for b in range(NT):
        enter_s[b] = jnp.broadcast_to(entering[b], (SUB, LN))
        entering.append(summ[b, 0:1] * entering[b] + summ[b, 1:2])
    following = zero
    for b in reversed(range(NT)):
        follow_s[b] = jnp.broadcast_to(following, (SUB, LN))
        following = summ[b, 2:3] * following + summ[b, 3:4] + summ[b, 4:5] * entering[b]
    e_me, f_me = enter_s[me], follow_s[me]
    for i in range(steps):
        x_s[pl.ds(i, SUB, stride=steps), :] = parts[0, i] + parts[1, i] * e_me + parts[2, i] * f_me
    sm_all[j, rows(me, frames), :] = x_s[...].astype(BF16)

    def block(g, b):
        return sm_all.at[g, rows(b, frames), :]

    def z_at(d):
        return peer(z, d, NZ) * CORES + core

    def send_z(d):
        return remote(block(j, me), block(j, me), sa_ss.at[d], sm_rs.at[me, j], tm=z_at(d))

    def send_n(dz, d):
        b = z_at(dz)
        return remote(block(j, b), block(j, b), sb_ss.at[dz, d], sm_rs.at[b, j], nn=nn_at(d))

    def send_c(dz, d):
        b, g = z_at(dz), nn_at(d)
        return remote(block(g, b), block(g, b), sc_ss.at[dz, d], sm_rs.at[b, g], tm=partner)

    def arrive(b, g):
        remote(block(g, b), block(g, b), sa_ss.at[0], sm_rs.at[b, g], tm=partner).wait_recv()

    def turn(b, g):
        sm_t[g, :, rows(b, frames)] = sm_all[g, rows(b, frames), :].T

    for d in range(1, NZ):
        send_z(d).start()
    send_obs(range(early, smax))
    for dz in range(NZ):
        if dz > 0:
            arrive(z_at(dz), j)
        for d in range(1, NN):
            send_n(dz, d).start()
        send_c(dz, 0).start()
        turn(z_at(dz), j)
    for dz in range(NZ):
        for d in range(1, NN):
            g = nn_at(d)
            arrive(z_at(dz), g)
            send_c(dz, d).start()
            turn(z_at(dz), g)
    for dz in range(NZ):
        for d in range(NN):
            b = peer(z, dz, NZ) * CORES + 1 - core
            arrive(b, nn_at(d))
            turn(b, nn_at(d))

    scale = 1.0 / math.sqrt(frames * NT)
    for s in range(smax):
        guarded(
            s,
            me,
            lambda: obs_all.__setitem__(
                (s, rows(me, frames), slice(None)), obs_ref[:, cols(first(me) + s)]
            ),
        )

    def out_copy(s, d):
        o = tm_at(d)
        return remote(
            out_s.at[s, rows(o, LO), :],
            out_ref.at[:, cols(first(me) + s)],
            out_ss.at[d, s],
            out_rs.at[me, s],
            tm=o,
        )

    def slot(s):
        r = first(me) + s
        for d in range(1, NT):
            o = tm_at(d)
            there = obs_all.at[s, rows(o, frames), :]
            remote(there, there, obs_ss.at[d, s], obs_rs.at[o, s], tm=o).wait_recv()
        eff = jnp.concatenate([effective(g, r) for g in range(groups)], axis=0).astype(BF16)
        smooth = jnp.concatenate([sm_all[g] for g in range(NN)], axis=1)
        rebuilt = jnp.dot(smooth, eff, preferred_element_type=F32)
        residual = ((obs_all[s].astype(F32) - rebuilt) * prec_ref[pl.ds(r, 1), :]).astype(BF16)
        smooth_t = sm_t[...].reshape(latents, NT * frames)
        summed = jnp.dot(smooth_t, residual, preferred_element_type=F32) * scale
        for g in range(groups):
            out_s[s, pl.ds(g * LATENT_GROUP, LATENT_GROUP), :] = (
                summed[g * LATENT_GROUP : (g + 1) * LATENT_GROUP] * mask_value(g, r)
            ).astype(BF16)
        for d in range(1, NT):
            out_copy(s, d).start()
        out_ref[:, cols(r)] = out_s[s, rows(me, LO), :]

    for s in range(smax):
        guarded(s, me, lambda: slot(s))

    for s in range(smax):
        for d in range(1, NT):
            o = tm_at(d)

            def landed():
                there = out_ref.at[:, cols(first(o) + s)]
                remote(there, there, out_ss.at[d, s], out_rs.at[o, s], tm=o).wait_recv()

            guarded(s, o, landed)

    for d in range(1, NT):
        summ_copy(d).wait_send()
        for s in range(smax):
            guarded(s, tm_at(d), lambda: obs_copy(s, d).wait_send())
            guarded(s, me, lambda: out_copy(s, d).wait_send())
    for d in range(1, NN):
        drv_copy(d).wait_send()
    for d in range(1, NZ):
        send_z(d).wait_send()
    for dz in range(NZ):
        for d in range(1, NN):
            send_n(dz, d).wait_send()
        for d in range(NN):
            send_c(dz, d).wait_send()


def per_device(NT, NN, observations, loadings, region_mask, precision, decay_rate, smoothing_lag):
    frames, neurons = observations.shape
    latents = loadings.shape[0]
    regions = region_mask.shape[1]
    LN, LO, NZ = latents // NN, latents // NT, NT // CORES
    smax = -(-regions // NT)
    steps = frames // SUB
    per = 5 if regions % 5 == 0 else 1
    dma = pltpu.SemaphoreType.DMA
    hbm = pl.BlockSpec(memory_space=pltpu.HBM)
    return pl.pallas_call(
        functools.partial(kernel, NT, NN),
        out_shape=jax.ShapeDtypeStruct((LO, neurons), BF16),
        in_specs=[hbm] * 6,
        out_specs=pl.BlockSpec(memory_space=pltpu.VMEM),
        scratch_shapes=[
            pltpu.VMEM((frames, neurons), BF16),
            pltpu.VMEM((latents, neurons), BF16),
            pltpu.SMEM(region_mask.shape, jnp.int32),
            pltpu.VMEM((regions, REGION), F32),
            pltpu.VMEM((frames, latents), BF16),
            pltpu.VMEM((1, latents), F32),
            dma((5,)),
            dma((regions // per,)),
            pltpu.VMEM((smax, NT * frames, REGION), BF16),
            pltpu.VMEM((latents, per * REGION), BF16),
            pltpu.VMEM((frames, latents), F32),
            pltpu.VMEM((NN, frames, LN), BF16),
            pltpu.VMEM((NN, frames, LN), BF16),
            pltpu.VMEM((frames, LN), F32),
            pltpu.VMEM((frames, LN), F32),
            pltpu.VMEM((frames, LN), F32),
            pltpu.VMEM((3, steps, SUB, LN), F32),
            pltpu.VMEM((NT, SUB, LN), F32),
            pltpu.VMEM((NT, SUB, LN), F32),
            pltpu.VMEM((NT, SUB, LN), F32),
            pltpu.VMEM((NN, NT * frames, LN), BF16),
            pltpu.VMEM((NN, LN, NT * frames), BF16),
            pltpu.VMEM((smax, latents, REGION), BF16),
            dma((NT, smax)),
            dma((NT, smax)),
            dma((NN,)),
            dma((NN,)),
            dma((NT,)),
            dma((NT,)),
            dma((NZ,)),
            dma((NZ, NN)),
            dma((NZ, NN)),
            dma((NT, NN)),
            dma((NT, smax)),
            dma((NT, smax)),
        ],
        compiler_params=pltpu.CompilerParams(
            collective_id=0, has_side_effects=True, vmem_limit_bytes=63 * 1024 * 1024
        ),
    )(
        observations,
        loadings,
        region_mask,
        precision.reshape(regions, REGION),
        decay_rate,
        smoothing_lag.reshape(1, latents),
    )


def solution(mesh):
    return jax.shard_map(
        functools.partial(per_device, mesh.shape["tm"], mesh.shape["neuron"]),
        mesh=mesh,
        in_specs=(
            P("tm", "neuron"),
            P(None, "neuron"),
            P(None, "neuron"),
            P("neuron"),
            P("tm", None),
            P(),
        ),
        out_specs=P("tm", "neuron"),
        check_vma=False,
    )
```
